512 devices in a mesh: row: 32 (over z, core), col: 16 (over x, y).
Axes of the slice: x: 4, y: 4, z: 16, core: 2. Of those that a mesh axis runs over, the one named last changes fastest.
Arguments:
- matrix: float32 [8192, 8192], P('row', 'col'), may hold values from -6 to 6
- pivots: int32 [3, 256], replicated, may hold values from 0 to 8191, as said below
- inverses: float32 [3, 256, 256], replicated, may hold values from -0.0234375 to 0.0234375
Outputs:
- factored: float32 [8192, 8192], P('row', 'col')
The draws below stay inside these ranges and needn't reach their ends.
Inputs may be any that keep to these rules, and one draw needn't show every extreme that they name: For panel k and position i, pivots[k, i] is either k * 256 + i or a row of index (k + 1) * 256 or more; position 0 of every panel is k * 256; no row is named twice within one panel; every panel names row 8191.
All inputs are finite; a program needn't handle non-finite values.
Results may differ from the reference program's by a relative error of at most 0.00017.
Values sent between devices are 32-bit elements; how exact they have to be, the bound alone decides.
A program may use at most 64 MiB of HBM per device.

```python
import jax
import jax.numpy as jnp
from jax import lax

NB = 256
R_DEV = 256
C_DEV = 512
PANELS = 3
ROWS = 8192
COLS = 8192
N_ROW = 32
N_COL = 16


def draw_pivots(key, part):
    panels = []
    offsets = jnp.arange(NB, dtype=jnp.int32)
    for panel in range(PANELS):
        subkey = jax.random.fold_in(key, 11 + panel)
        key_perm, key_spot, key_stay = jax.random.split(subkey, 3)
        start = (panel + 1) * NB
        count = ROWS - start - 1
        picks = jax.random.permutation(key_perm, count)[:NB].astype(jnp.int32) + start
        spot = jax.random.randint(key_spot, (), 1, NB)
        picks = jnp.where(offsets == spot, ROWS - 1, picks)
        stay = ((jax.random.randint(key_stay, (NB,), 0, 4) == 0) | (offsets == 0)) & (offsets != spot)
        panels.append(jnp.where(stay, panel * NB + offsets, picks).astype(jnp.int32))
    return jnp.stack(panels)


def levels(rng, dims, cuts, low, high):
    gain = 1.0
    for axis_at, shards_of in cuts:
        draws = jax.random.uniform(jax.random.fold_in(jax.random.fold_in(rng, 6), axis_at), (shards_of,), jnp.float32, low / len(cuts), high / len(cuts))
        gain = gain * jnp.repeat(jnp.exp(draws), dims[axis_at] // shards_of).reshape((-1,) + (1,) * (len(dims) - 1 - axis_at))
    return gain


def normal_values(key, dims, spread, most, pieces=(), kind=jnp.bfloat16):
    values = spread * jax.random.normal(key, dims, jnp.float32)
    if pieces:
        values = values * levels(key, dims, pieces, -0.22, 0.18)
    return jnp.clip(values, -most, most).astype(kind)


def setup_inputs(seed: int = 0) -> dict:
    key_of = jax.random.split(jax.random.key(seed), 4)
    return {
        "matrix": normal_values(key_of[0], (ROWS, COLS), 1.0, 6.0, ((0, 32), (1, 16)), jnp.float32),
        "pivots": draw_pivots(jax.random.fold_in(key_of[3], 71), 0),
        "inverses": normal_values(key_of[2], (PANELS, NB, NB), (NB * NB) ** -0.5, 0.0234375, (), jnp.float32),
    }


def to_logical(stored):
    row_blocks = R_DEV // NB
    col_blocks = C_DEV // NB
    shaped = stored.reshape(N_ROW, row_blocks, NB, N_COL, col_blocks, NB)
    return shaped.transpose(1, 0, 2, 4, 3, 5).reshape(ROWS, COLS)


def to_stored(logical):
    row_blocks = R_DEV // NB
    col_blocks = C_DEV // NB
    shaped = logical.reshape(row_blocks, N_ROW, NB, col_blocks, N_COL, NB)
    return shaped.transpose(1, 0, 2, 4, 3, 5).reshape(ROWS, COLS)


def reference(matrix, pivots, inverses):
    grid = to_logical(matrix)
    offsets = jnp.arange(NB, dtype=jnp.int32)
    for panel in range(PANELS):
        top = panel * NB
        chosen = pivots[panel]
        tops = top + offsets
        stay = chosen == tops
        upper = grid[chosen]
        displaced = grid[top:top + NB]
        grid = grid.at[jnp.where(stay, tops, chosen)].set(displaced)
        grid = grid.at[top:top + NB].set(upper)
        lower = top + NB
        strip = grid[lower:, top:top + NB]
        factor = jnp.dot(strip, inverses[panel], precision=lax.Precision.HIGHEST, preferred_element_type=jnp.float32)
        grid = grid.at[lower:, top:top + NB].set(factor)
        urow = grid[top:top + NB, lower:]
        trailing = grid[lower:, lower:] - jnp.dot(factor, urow, precision=lax.Precision.HIGHEST, preferred_element_type=jnp.float32)
        grid = grid.at[lower:, lower:].set(trailing)
    return to_stored(grid)
```

```python
import functools

import jax
import jax.numpy as jnp
from jax import lax
from jax.experimental import pallas as pl
from jax.experimental.pallas import tpu as pltpu
from jax.sharding import PartitionSpec as P

MESH = pl.DeviceIdType.MESH
F32 = jnp.float32
BF16 = jnp.bfloat16
NX, NY = 4, 4


def dot(a, b):
    return jnp.dot(a, b, preferred_element_type=F32)


def split2(a):
    hi = a.astype(BF16)
    return hi, (a - hi.astype(F32)).astype(BF16)


def split3(a):
    hi = a.astype(BF16)
    rest = a - hi.astype(F32)
    mid = rest.astype(BF16)
    return hi, mid, (rest - mid.astype(F32)).astype(BF16)


def mm(a, b):
    ah, al = split2(a)
    bh, bl = split2(b)
    return dot(ah, bh) + (dot(ah, bl) + dot(al, bh))


def select_rows(onehot, b):
    hi, mid, lo = split3(b)
    return dot(onehot, hi) + dot(onehot, mid) + dot(onehot, lo)


def kernel(
    nz, nb,
    a_ref, piv_ref, inv_ref, o_ref,
    B, Pt, SG, DG, TG, XG, NBf, rp, rm, sp, sm, Y,
    ex_s, ex_r, ds_s, ds_r, rs_s, rs_r, dg_s, dg_r, sg_s, sg_r, tg_s, tg_r, fw_s, fw_r,
    t1_s, t1_r, t2_s, t2_r, x1_s, x1_r, x2_s, x2_r, x3_s, x3_r, out_s, out_r,
):
    row = lax.axis_index("row")
    q = lax.axis_index("col")
    z, c = row // 2, row % 2
    x, y = q // NY, q % NY
    ch = nb // nz
    up, down = 2 * ((z + 1) % nz) + c, 2 * ((z + nz - 1) % nz) + c
    sib = 2 * z + 1 - c
    source = jnp.logical_and(jnp.logical_and(x == 0, y < 3), c == 0)

    def dev(r, k):
        return {"row": r, "col": k}

    def remote(src, dst, ss, rs, r, k):
        return pltpu.make_async_remote_copy(
            src_ref=src, dst_ref=dst, send_sem=ss, recv_sem=rs,
            device_id=dev(r, k), device_id_type=MESH,
        )

    bar = pltpu.get_barrier_semaphore()

    def greet(r, k):
        pl.semaphore_signal(bar, inc=1, device_id=dev(r, k), device_id_type=MESH)

    greet(sib, q)
    greet(up, q)
    greet(down, q)
    for d in range(1, NY):
        greet(row, x * NY + (y + d) % NY)

    @pl.when(z != 0)
    def _():
        greet(c, q)

    @pl.when(z != 1)
    def _():
        greet(2 + c, q)

    @pl.when(jnp.logical_and(x != 0, y < 3))
    def _():
        greet(2 * z, y)

    expected = (
        3 + (NY - 1)
        + jnp.where(z <= 1, nz - 1, 0)
        + jnp.where(source, 2 * (NX - 1), 0)
    )
    pl.semaphore_wait(bar, expected)

    other = pl.multiple_of((1 - c) * nb, nb)
    mine = pl.multiple_of(c * nb, nb)
    swap = remote(a_ref.at[:, pl.ds(other, nb)], B.at[c], ex_s, ex_r, sib, q)
    swap.start()
    B[c] = a_ref[:, pl.ds(mine, nb)]

    lane = lax.broadcasted_iota(jnp.int32, (nb, nb), 1)
    subl = lax.broadcasted_iota(jnp.int32, (nb, nb), 0)
    prow = [piv_ref[k:k + 1, :].astype(F32) for k in range(3)]
    eye = lane == subl
    pcol = [
        jnp.max(jnp.where(eye, jnp.broadcast_to(p, (nb, nb)), -1.0), axis=1, keepdims=True)
        for p in prow
    ]
    lanef = lane.astype(F32)

    def back(v, k):
        n = v.shape[0]
        hit = jnp.where(
            jnp.broadcast_to(v, (n, nb)) == jnp.broadcast_to(prow[k], (n, nb)),
            lanef[:1, :] + float(k * nb), -1.0,
        )
        best = jnp.max(hit, axis=1, keepdims=True)
        return jnp.where(best >= 0.0, best, v)

    slots = [pcol[0], back(pcol[1], 0), back(back(pcol[2], 1), 0)]
    base = (z * 2 * nb).astype(F32)
    own = [
        subl[:, :1].astype(F32) + base + float(h * nb) for h in range(2)
    ]
    came = [back(back(back(g, 2), 1), 0) for g in own]
    here = lax.broadcasted_iota(jnp.int32, (nb, 2 * nb), 1).astype(F32) + base

    swap.wait()

    def share(d):
        to = (z + d) % nz
        rows = pl.ds(pl.multiple_of(to * ch, ch), ch)
        return to, rows

    @pl.when(z == 0)
    def _():
        for d in range(1, nz):
            to, rows = share(d)
            remote(B.at[:, rows], DG.at[pl.ds(0, 2), rows], ds_s.at[d], ds_r.at[0], 2 * to + c, q).start()
        DG[0:2, 0:ch] = B[:, 0:ch]

    @pl.when(z == 1)
    def _():
        for d in range(1, nz):
            to, rows = share(d)
            remote(
                B.at[pl.ds(0, 1), rows], DG.at[pl.ds(2, 1), rows], ds_s.at[d], ds_r.at[1], 2 * to + c, q
            ).start()
        DG[2, ch:2 * ch] = B[0, ch:2 * ch]

    parts = split3(B[...].reshape(2 * nb, nb))
    for k in range(3):
        oh = (jnp.broadcast_to(slots[k], (nb, 2 * nb)) == here).astype(F32).astype(BF16)
        Pt[k] = dot(oh, parts[0]) + dot(oh, parts[1]) + dot(oh, parts[2])

    def chunk(i):
        return pl.ds(pl.multiple_of(lax.rem(i + 2 * nz, nz) * ch, ch), ch)

    half = nz // 2

    def rs_step(t):
        rows = chunk(z + half - t)
        sp[t] = Pt[:, rows] if t == 0 else Pt[:, rows] + rp[t - 1]
        cps = [remote(sp.at[t], rp.at[t], rs_s.at[0], rs_r.at[0, t], up, q)]
        if t < half - 1:
            rows = chunk(z - (half - 1) + t)
            sm[t] = Pt[:, rows] if t == 0 else Pt[:, rows] + rm[t - 1]
            cps.append(remote(sm.at[t], rm.at[t], rs_s.at[1], rs_r.at[1, t], down, q))
        for cp in cps:
            cp.start()
        return cps

    def ag_step(buf, t, ss, rs):
        rows = chunk(z - t)
        cps = [remote(buf.at[:, rows], buf.at[:, rows], ss.at[0], rs.at[0, t], up, q)]
        if t < half - 1:
            rows = chunk(z + t)
            cps.append(remote(buf.at[:, rows], buf.at[:, rows], ss.at[1], rs.at[1, t], down, q))
        for cp in cps:
            cp.start()
        return cps

    tmine = TG.at[pl.ds(3 * c, 3)]

    def fwd(slot, i):
        rows = chunk(i)
        cp = remote(tmine.at[:, rows], tmine.at[:, rows], fw_s.at[slot], fw_r.at[slot], sib, q)
        cp.start()
        return cp

    forwards = []
    lag_d = min(3, half - 1)
    lag_s = half
    lag_t = half + lag_d
    for tick in range(lag_t + half):
        cps = []
        if tick < half:
            cps += rs_step(tick)
        if tick == lag_d:
            @pl.when(z == 0)
            def _():
                for d in range(1, nz):
                    to, rows = share(d)
                    remote(
                        B.at[:, rows], DG.at[pl.ds(0, 2), rows], ds_s.at[d], ds_r.at[0], 2 * to + c, q
                    ).wait_send()

            @pl.when(z == 1)
            def _():
                for d in range(1, nz):
                    to, rows = share(d)
                    remote(
                        B.at[pl.ds(0, 1), rows], DG.at[pl.ds(2, 1), rows], ds_s.at[d], ds_r.at[1], 2 * to + c, q
                    ).wait_send()

            rows = chunk(z)

            @pl.when(z != 0)
            def _():
                remote(B.at[:, rows], DG.at[pl.ds(0, 2), rows], ds_s.at[0], ds_r.at[0], up, q).wait_recv()

            @pl.when(z != 1)
            def _():
                remote(
                    B.at[pl.ds(0, 1), rows], DG.at[pl.ds(2, 1), rows], ds_s.at[0], ds_r.at[1], up, q
                ).wait_recv()
        if lag_d <= tick < lag_d + half:
            cps += ag_step(DG, tick - lag_d, dg_s, dg_r)
        if tick == lag_s:
            rows = chunk(z)
            total = Pt[:, rows] + rp[half - 1] + rm[half - 2]
            SG[:, rows] = total

            @pl.when(source)
            def _():
                first = jnp.where(y == 0, 1, 0)
                second = jnp.where(y == 2, 1, 2)
                for d in range(1, NX):
                    remote(SG.at[first, rows], TG.at[y, rows], t1_s.at[0, d], t1_r, 2 * z, d * NY + y).start()
                for d in range(NX):
                    remote(
                        SG.at[second, rows], TG.at[3 + y, rows], t1_s.at[1, d], t1_r, 2 * z + 1, d * NY + y
                    ).start()
                TG[y, rows] = SG[first, rows]
        if lag_s <= tick < lag_s + half:
            cps += ag_step(SG, tick - lag_s, sg_s, sg_r)
        if tick == lag_s + 1:

            @pl.when(y < 3)
            def _():
                rows = chunk(z)
                piece = TG.at[3 * c + y, rows]

                @pl.when(jnp.logical_not(source))
                def _():
                    remote(piece, piece, t1_s.at[0, 0], t1_r, row, y).wait_recv()

                for d in range(1, NY):
                    remote(piece, piece, t2_s.at[d], t2_r.at[y], row, x * NY + (y + d) % NY).start()

        if tick == lag_t:
            rows = chunk(z)
            for j in range(3):
                @pl.when(y != j)
                def _(j=j):
                    piece = TG.at[3 * c + j, rows]
                    remote(piece, piece, t2_s.at[0], t2_r.at[j], row, q).wait_recv()
            forwards.append(fwd(0, z))
            dg = split3(DG[...].reshape(3 * nb, nb))
            there = lax.broadcasted_iota(jnp.int32, (nb, 3 * nb), 1).astype(F32)
            for h in range(2):
                oh = (jnp.broadcast_to(came[h], (nb, 3 * nb)) == there).astype(F32).astype(BF16)
                moved = dot(oh, dg[0]) + dot(oh, dg[1]) + dot(oh, dg[2])
                keep = jnp.broadcast_to(came[h], (nb, nb)) == jnp.broadcast_to(own[h], (nb, nb))
                NBf[h] = jnp.where(keep, B[h], moved)

            @pl.when(source)
            def _():
                for d in range(1, NX):
                    remote(NBf.at[0], XG.at[y, 0], x1_s.at[0, d], x1_r, 2 * z, d * NY + y).start()
                for d in range(NX):
                    remote(NBf.at[1], XG.at[y, 1], x1_s.at[1, d], x1_r, 2 * z + 1, d * NY + y).start()
                XG[y, 0] = NBf[0]
        if tick >= lag_t:
            cps += ag_step(tmine, tick - lag_t, tg_s, tg_r)
        if tick == lag_t + min(3, half - 2):
            @pl.when(y < 3)
            def _():
                piece = XG.at[y, c]

                @pl.when(jnp.logical_not(source))
                def _():
                    remote(piece, piece, x1_s.at[0, 0], x1_r, row, y).wait_recv()

                for d in range(1, NY):
                    remote(piece, piece, x2_s.at[d], x2_r.at[y], row, x * NY + (y + d) % NY).start()
        for cp in cps:
            cp.wait()
        if tick >= lag_t:
            t = tick - lag_t
            forwards.append(fwd(1 + t, z - 1 - t))
            if t < half - 1:
                forwards.append(fwd(1 + half + t, z + 1 + t))

    for j in range(3):
        @pl.when(y != j)
        def _(j=j):
            piece = XG.at[j, c]
            remote(piece, piece, x2_s.at[0], x2_r.at[j], row, q).wait_recv()
    strips = remote(XG.at[:, c], XG.at[:, c], x3_s, x3_r, sib, q)
    strips.start()
    strips.wait()
    for cp in forwards:
        cp.wait()

    i0, i1, i2 = inv_ref[0], inv_ref[1], inv_ref[2]
    t10, t01, t02, t20, t21, t12 = (TG[j] for j in range(6))
    l10, l20 = mm(t10, i0), mm(t20, i0)
    l21 = mm(t21 - mm(l20, t01), i1)
    u12 = t12 - mm(l10, t02)
    u0 = SG[0]
    u1 = SG[1] - mm(l10, u0)
    u2 = SG[2] - mm(l20, u0) - mm(l21, u1)
    panel_col = jnp.logical_and(c == 0, q < 3)
    for h in range(2):
        l0 = mm(XG[0, h], i0)
        l1 = mm(XG[1, h] - mm(l0, t01), i1)
        l2 = mm(XG[2, h] - mm(l0, t02) - mm(l1, u12), i2)
        Y[h] = NBf[h] - mm(l0, u0) - mm(l1, u1) - mm(l2, u2)
        for k, l in enumerate((l0, l1, l2)):
            @pl.when(jnp.logical_and(panel_col, q == k))
            def _(h=h, l=l):
                Y[h] = l
        for r, u in enumerate((u0, u1, u2)):
            if r % 2 != h:
                continue

            @pl.when(row // 2 * 2 + h == r)
            def _(h=h, u=u):
                Y[h] = u
        for r, k, l in ((1, 0, l10), (2, 0, l20), (2, 1, l21)):
            if r % 2 != h:
                continue

            @pl.when(jnp.logical_and(row // 2 * 2 + h == r, jnp.logical_and(panel_col, q == k)))
            def _(h=h, l=l):
                Y[h] = l

    back_copy = remote(Y.at[1 - c], o_ref.at[:, pl.ds(mine, nb)], out_s, out_r, sib, q)
    back_copy.start()
    o_ref[:, pl.ds(mine, nb)] = Y[c]
    back_copy.wait()

    @pl.when(source)
    def _():
        rows = chunk(z)
        for d in range(1, NX):
            remote(SG.at[0, rows], TG.at[y, rows], t1_s.at[0, d], t1_r, 2 * z, d * NY + y).wait_send()
            remote(NBf.at[0], XG.at[y, 0], x1_s.at[0, d], x1_r, 2 * z, d * NY + y).wait_send()
        for d in range(NX):
            remote(SG.at[0, rows], TG.at[3 + y, rows], t1_s.at[1, d], t1_r, 2 * z + 1, d * NY + y).wait_send()
            remote(NBf.at[1], XG.at[y, 1], x1_s.at[1, d], x1_r, 2 * z + 1, d * NY + y).wait_send()

    @pl.when(y < 3)
    def _():
        rows = chunk(z)
        for d in range(1, NY):
            to = x * NY + (y + d) % NY
            piece = TG.at[3 * c + y, rows]
            remote(piece, piece, t2_s.at[d], t2_r.at[y], row, to).wait_send()
            piece = XG.at[y, c]
            remote(piece, piece, x2_s.at[d], x2_r.at[y], row, to).wait_send()


def on_device(matrix, pivots, inverses):
    nb = inverses.shape[1]
    nz = lax.axis_size("row") // 2
    ch = nb // nz
    half = nz // 2
    DMA = pltpu.SemaphoreType.DMA

    def vm(*shape):
        return pltpu.VMEM(shape, F32)

    return pl.pallas_call(
        functools.partial(kernel, nz, nb),
        out_shape=jax.ShapeDtypeStruct(matrix.shape, matrix.dtype),
        in_specs=[pl.BlockSpec(memory_space=pltpu.VMEM)] * 3,
        out_specs=pl.BlockSpec(memory_space=pltpu.VMEM),
        scratch_shapes=[
            vm(2, nb, nb), vm(3, nb, nb), vm(3, nb, nb), vm(3, nb, nb), vm(6, nb, nb),
            vm(3, 2, nb, nb), vm(2, nb, nb),
            vm(half, 3, ch, nb), vm(half - 1, 3, ch, nb), vm(half, 3, ch, nb), vm(half - 1, 3, ch, nb),
            vm(2, nb, nb),
            DMA, DMA, DMA((nz,)), DMA((2,)),
            DMA((2,)), DMA((2, half)), DMA((2,)), DMA((2, half)),
            DMA((2,)), DMA((2, half)), DMA((2,)), DMA((2, half)),
            DMA((2 * half,)), DMA((2 * half,)),
            DMA((2, NX)), DMA, DMA((NY,)), DMA((3,)),
            DMA((2, NX)), DMA, DMA((NY,)), DMA((3,)),
            DMA, DMA, DMA, DMA,
        ],
        compiler_params=pltpu.CompilerParams(
            collective_id=0, has_side_effects=True, vmem_limit_bytes=48 * 2**20
        ),
        name="panels",
    )(matrix, pivots, inverses)


def solution(mesh):
    placed = (P("row", "col"), P(), P())
    return jax.shard_map(
        on_device, mesh=mesh, in_specs=placed, out_specs=P("row", "col"), check_vma=False
    )
```

```python
import functools

import jax
import jax.numpy as jnp
from jax import lax
from jax.experimental import pallas as pl
from jax.experimental.pallas import tpu as pltpu
from jax.sharding import PartitionSpec as P

MESH = pl.DeviceIdType.MESH
F32 = jnp.float32
BF16 = jnp.bfloat16
NX, NY = 4, 4
RING = ((0, 1, 2, 3, 4, 5, 6, 7, 8), (0, -1, -2, -3, -4, -5, -6, -7))
RS_WAY, D_WAY, S_WAY, T_WAY = RING, RING, RING, RING
AT_D, AT_S, AT_T2, AT_T, AT_X2 = 4, 8, 9, 10, 15
PER, PX = 5, 2


def dot(a, b):
    return jnp.dot(a, b, preferred_element_type=F32)


def split2(a):
    hi = a.astype(BF16)
    return hi, (a - hi.astype(F32)).astype(BF16)


def split3(a):
    hi = a.astype(BF16)
    rest = a - hi.astype(F32)
    mid = rest.astype(BF16)
    return hi, mid, (rest - mid.astype(F32)).astype(BF16)


def mm(a, b):
    ah, al = split2(a)
    bh, bl = split2(b)
    return dot(ah, bh) + (dot(ah, bl) + dot(al, bh))


def select_rows(onehot, b):
    hi, mid, lo = split3(b)
    return dot(onehot, hi) + dot(onehot, mid) + dot(onehot, lo)


def kernel(
    nz, nb,
    a_ref, piv_hbm, inv_hbm, o_ref,
    piv_ref, inv_ref, sm_s,
    B, Pt, SG, DG, TG, XG, NBf, NX_, got, put,
    ld_s, ex_s, ex_r, ds_s, ds_r, rs_s, rs_r, dg_s, dg_r, sg_s, sg_r, tg_s, tg_r, ft_s, ft_r, fs_s, fs_r,
    t1_s, t1_r, t2_s, t2_r, x1_s, x1_r, x2_s, x2_r, nx_s, nx_r,
):
    row = lax.axis_index("row")
    q = lax.axis_index("col")
    z, c = row // 2, row % 2
    x, y = q // NY, q % NY
    ch = nb // nz
    up = 2 * ((z + 1) % nz) + c
    sib = 2 * z + 1 - c
    source = jnp.logical_and(jnp.logical_and(x == 0, y < 3), c == 0)

    def dev(r, k):
        return {"row": r, "col": k}

    def remote(src, dst, ss, rs, r, k):
        return pltpu.make_async_remote_copy(
            src_ref=src, dst_ref=dst, send_sem=ss, recv_sem=rs,
            device_id=dev(r, k), device_id_type=MESH,
        )

    other = pl.multiple_of((1 - c) * nb, nb)
    mine = pl.multiple_of(c * nb, nb)
    load = pltpu.make_async_copy(a_ref.at[:, pl.ds(mine, nb)], B.at[c], ld_s)
    load.start()
    load_piv = pltpu.make_async_copy(piv_hbm, piv_ref, sm_s.at[0])
    load_inv = pltpu.make_async_copy(inv_hbm, inv_ref, sm_s.at[1])
    load_piv.start()
    load_inv.start()

    bar = pltpu.get_barrier_semaphore()

    def greet(r, k):
        pl.semaphore_signal(bar, inc=1, device_id=dev(r, k), device_id_type=MESH)

    greet(sib, q)
    for d in (1, 2, nz - 1, nz - 2):
        greet(2 * ((z + d) % nz) + c, q)
    for d in range(1, NY):
        greet(row, x * NY + (y + d) % NY)

    @pl.when(z != 0)
    def _():
        greet(c, q)

    @pl.when(z != 1)
    def _():
        greet(2 + c, q)

    @pl.when(jnp.logical_and(x != 0, y < 3))
    def _():
        greet(2 * z, y)

    expected = (
        5 + (NY - 1)
        + jnp.where(z <= 1, nz - 1, 0)
        + jnp.where(source, 2 * (NX - 1), 0)
    )
    pl.semaphore_wait(bar, expected)
    swap = remote(a_ref.at[:, pl.ds(other, nb)], B.at[c], ex_s, ex_r, sib, q)
    swap.start()
    load_piv.wait()
    lane = lax.broadcasted_iota(jnp.int32, (nb, nb), 1)
    subl = lax.broadcasted_iota(jnp.int32, (nb, nb), 0)
    prow = [piv_ref[k:k + 1, :].astype(F32) for k in range(3)]
    eye = lane == subl
    pcol = [
        jnp.max(jnp.where(eye, jnp.broadcast_to(p, (nb, nb)), -1.0), axis=1, keepdims=True)
        for p in prow
    ]
    lanef = lane.astype(F32)

    def back(v, k):
        n = v.shape[0]
        hit = jnp.where(
            jnp.broadcast_to(v, (n, nb)) == jnp.broadcast_to(prow[k], (n, nb)),
            lanef[:1, :] + float(k * nb), -1.0,
        )
        best = jnp.max(hit, axis=1, keepdims=True)
        return jnp.where(best >= 0.0, best, v)

    slots = [pcol[0], back(pcol[1], 0), back(back(pcol[2], 1), 0)]
    base = (z * 2 * nb).astype(F32)
    own = [subl[:, :1].astype(F32) + base + float(h * nb) for h in range(2)]
    came = [back(back(back(g, 2), 1), 0) for g in own]
    here = lax.broadcasted_iota(jnp.int32, (nb, 2 * nb), 1).astype(F32) + base

    load.wait()
    swap.wait_recv()

    def ring(i):
        return lax.rem(i + 2 * nz, nz)

    def share(which, d):
        i = ring(z + d)
        rows = pl.ds(pl.multiple_of(i * ch, ch), ch)
        if which == 0:
            return remote(B.at[:, rows], DG.at[i, pl.ds(0, 2)], ds_s.at[d], ds_r.at[0], 2 * i + c, q)
        return remote(B.at[pl.ds(0, 1), rows], DG.at[i, pl.ds(2, 1)], ds_s.at[d], ds_r.at[1], 2 * i + c, q)

    far_first = sorted(range(1, nz), key=lambda d: -min(d, nz - d))

    @pl.when(z == 0)
    def _():
        DG[0, 0:2] = B[:, 0:ch]

    @pl.when(z == 1)
    def _():
        DG[1, 2] = B[0, ch:2 * ch]

    parts = split3(B[...].reshape(2 * nb, nb))
    for k in range(3):
        oh = (jnp.broadcast_to(slots[k], (nb, 2 * nb)) == here).astype(F32).astype(BF16)
        part = dot(oh, parts[0]) + dot(oh, parts[1]) + dot(oh, parts[2])
        Pt[:, k] = part.reshape(nz, ch, nb)

    sent = []
    def begin(cp):
        cp.start()
        sent.append(cp)
        return cp

    flight = {}

    def chip(d):
        return 2 * ring(z + d) + c

    def rs_step(t):
        for w, route in enumerate(RS_WAY):
            n = len(route) - 1
            at = sum(len(r) - 1 for r in RS_WAY[:w]) + t
            if 0 < t <= n:
                flight.pop(("rs", w)).wait_recv()
            if t < n:
                far = route[n - t]
                i = ring(z + far)
                put[at] = Pt[i] if t == 0 else Pt[i] + got[at - 1]
                flight["rs", w] = begin(
                    remote(put.at[at], got.at[at], rs_s.at[at], rs_r.at[at], chip(far - route[n - t - 1]), q)
                )

    def ag_step(name, way, buf, t, ss, rs, forward=None):
        if t == 0 and forward is not None:
            forward(0, z)
        for w, route in enumerate(way):
            n = len(route) - 1
            at = sum(len(r) - 1 for r in way[:w]) + t
            if 0 < t <= n:
                flight.pop((name, w)).wait_recv()
            if t < n:
                i = ring(z - route[t])
                flight[name, w] = begin(
                    remote(buf.at[i], buf.at[i], ss.at[at], rs.at[at], chip(route[t + 1] - route[t]), q)
                )
            if forward is not None and 0 < t <= n:
                forward(at, z - route[t])

    tmine = TG.at[c]
    smine = SG.at[c]
    crossing = []

    def to_sibling(buf, ss, rs):
        def forward(slot, i):
            i = ring(i)
            cp = begin(remote(buf.at[i], buf.at[i], ss.at[slot], rs.at[slot], sib, q))
            crossing.append(cp)
        return forward

    def part(p):
        return pl.ds(p * (nb // PX), nb // PX)

    def strips(p):
        for d in range(NX):
            for h in range(2):
                if d or h:
                    yield h, d, remote(
                        NBf.at[h, part(p)], XG.at[y, part(p)], x1_s.at[h, d, p], x1_r.at[p], 2 * z + h, d * NY + y
                    )

    def strips_y(d, p):
        piece = XG.at[y, part(p)]
        return remote(piece, piece, x2_s.at[d, p], x2_r.at[y, p], row, x * NY + (y + d) % NY)

    def rounds(way):
        return max(len(r) for r in way) - 1

    n_rs, n_d, n_s, n_t = rounds(RS_WAY), rounds(D_WAY), rounds(S_WAY), rounds(T_WAY)
    at_x = AT_D + n_d
    for tick in range(max(n_rs, AT_D + n_d, AT_S + n_s, AT_T + n_t, AT_X2) + 1):
        if tick <= n_rs:
            rs_step(tick)
        for which in range(2):
            @pl.when(z == which)
            def _(which=which):
                for d in far_first[tick * PER:(tick + 1) * PER]:
                    share(which, d).start()

        if tick == AT_S:
            total, at = Pt[z], -1
            for route in RS_WAY:
                at += len(route) - 1
                total += got[at]
            SG[c, z] = total

            @pl.when(source)
            def _():
                first = jnp.where(y == 0, 1, 0)
                second = jnp.where(y == 2, 1, 2)
                for d in range(1, NX):
                    remote(SG.at[0, z, first], TG.at[0, z, y], t1_s.at[0, d], t1_r, 2 * z, d * NY + y).start()
                for d in range(NX):
                    remote(
                        SG.at[0, z, second], TG.at[1, z, y], t1_s.at[1, d], t1_r, 2 * z + 1, d * NY + y
                    ).start()
                TG[0, z, y] = SG[0, z, first]
        if AT_S <= tick <= AT_S + n_s:
            ag_step("s", S_WAY, smine, tick - AT_S, sg_s, sg_r, to_sibling(smine, fs_s, fs_r))
        if tick == AT_T2:
            @pl.when(y < 3)
            def _():
                piece = TG.at[c, z, y]

                @pl.when(jnp.logical_not(source))
                def _():
                    remote(piece, piece, t1_s.at[0, 0], t1_r, row, y).wait_recv()

                for d in range(1, NY):
                    remote(piece, piece, t2_s.at[d], t2_r.at[y], row, x * NY + (y + d) % NY).start()

        if tick == AT_D:
            @pl.when(z != 0)
            def _():
                remote(B.at[:, 0:ch], DG.at[z, pl.ds(0, 2)], ds_s.at[0], ds_r.at[0], up, q).wait_recv()

            @pl.when(z != 1)
            def _():
                remote(
                    B.at[pl.ds(0, 1), 0:ch], DG.at[z, pl.ds(2, 1)], ds_s.at[0], ds_r.at[1], up, q
                ).wait_recv()
        if AT_D <= tick <= AT_D + n_d:
            ag_step("d", D_WAY, DG, tick - AT_D, dg_s, dg_r)
        if tick == AT_T:
            for j in range(3):
                @pl.when(y != j)
                def _(j=j):
                    piece = TG.at[c, z, j]
                    remote(piece, piece, t2_s.at[0], t2_r.at[j], row, q).wait_recv()
        if AT_T <= tick <= AT_T + n_t:
            ag_step("t", T_WAY, tmine, tick - AT_T, tg_s, tg_r, to_sibling(tmine, ft_s, ft_r))
        if tick == at_x:
            dg = [split3(DG[:, k].reshape(nb, nb)) for k in range(3)]
            for h in range(2):
                moved = jnp.zeros((nb, nb), F32)
                for k in range(3):
                    oh = jnp.broadcast_to(came[h], (nb, nb)) == lanef + float(k * nb)
                    oh = oh.astype(F32).astype(BF16)
                    moved += dot(oh, dg[k][0]) + dot(oh, dg[k][1]) + dot(oh, dg[k][2])
                keep = jnp.broadcast_to(came[h], (nb, nb)) == jnp.broadcast_to(own[h], (nb, nb))
                NBf[h] = jnp.where(keep, B[h], moved)

            @pl.when(source)
            def _():
                for p in range(PX):
                    for h, d, cp in strips(p):
                        cp.start()
                XG[y] = NBf[0]

            crossing.append(begin(remote(NBf.at[1 - c], NX_, nx_s, nx_r, sib, q)))
        if tick == AT_X2:
            @pl.when(y < 3)
            def _():
                for p in range(PX):
                    piece = XG.at[y, part(p)]

                    @pl.when(jnp.logical_not(source))
                    def _(p=p, piece=piece):
                        remote(piece, piece, x1_s.at[0, 0, p], x1_r.at[p], row, y).wait_recv()

                    for d in range(1, NY):
                        strips_y(d, p).start()

    for j in range(3):
        @pl.when(y != j)
        def _(j=j):
            for p in range(PX):
                piece = XG.at[j, part(p)]
                remote(piece, piece, x2_s.at[0, p], x2_r.at[j, p], row, q).wait_recv()
    for cp in crossing:
        cp.wait_recv()

    load_inv.wait()
    i0, i1, i2 = inv_ref[0], inv_ref[1], inv_ref[2]
    t10, t01, t02, t20, t21, t12 = (TG[j // 3, :, j % 3].reshape(nb, nb) for j in range(6))
    l10, l20 = mm(t10, i0), mm(t20, i0)
    l21 = mm(t21 - mm(l20, t01), i1)
    u12 = t12 - mm(l10, t02)
    l0 = mm(XG[0], i0)
    l1 = mm(XG[1] - mm(l0, t01), i1)
    l2 = mm(XG[2] - mm(l0, t02) - mm(l1, u12), i2)
    for h in range(2):
        cols = pl.ds(h * nb, nb)
        s0, s1, s2 = (SG[h, :, k].reshape(nb, nb) for k in range(3))
        u0 = s0
        u1 = s1 - mm(l10, u0)
        u2 = s2 - mm(l20, u0) - mm(l21, u1)

        @pl.when(row >= 3)
        def _(h=h, cols=cols, u0=u0, u1=u1, u2=u2):
            @pl.when(c == h)
            def _():
                o_ref[:, cols] = NBf[h]

            @pl.when(c != h)
            def _():
                o_ref[:, cols] = NX_[...]

            o_ref[:, cols] -= mm(l0, u0) + mm(l1, u1) + mm(l2, u2)

        for r, u in enumerate((u0, u1, u2)):
            @pl.when(row == r)
            def _(cols=cols, u=u):
                o_ref[:, cols] = u
    for k, l in enumerate((l0, l1, l2)):
        @pl.when(jnp.logical_and(row >= 3, q == k))
        def _(l=l):
            o_ref[:, 0:nb] = l
    for r, k, l in ((1, 0, l10), (2, 0, l20), (2, 1, l21)):
        @pl.when(jnp.logical_and(row == r, q == k))
        def _(l=l):
            o_ref[:, 0:nb] = l

    swap.wait_send()
    for cp in sent:
        cp.wait_send()
    for which in range(2):
        @pl.when(z == which)
        def _(which=which):
            for d in range(1, nz):
                share(which, d).wait_send()

    @pl.when(source)
    def _():
        for d in range(1, NX):
            remote(SG.at[0, z, 0], TG.at[0, z, y], t1_s.at[0, d], t1_r, 2 * z, d * NY + y).wait_send()
        for d in range(NX):
            remote(SG.at[0, z, 0], TG.at[1, z, y], t1_s.at[1, d], t1_r, 2 * z + 1, d * NY + y).wait_send()
        for p in range(PX):
            for h, d, cp in strips(p):
                cp.wait_send()

    @pl.when(y < 3)
    def _():
        for d in range(1, NY):
            to = x * NY + (y + d) % NY
            piece = TG.at[c, z, y]
            remote(piece, piece, t2_s.at[d], t2_r.at[y], row, to).wait_send()
            for p in range(PX):
                strips_y(d, p).wait_send()


def on_device(matrix, pivots, inverses):
    nb = inverses.shape[1]
    nz = lax.axis_size("row") // 2
    ch = nb // nz
    DMA = pltpu.SemaphoreType.DMA

    def vm(*shape):
        return pltpu.VMEM(shape, F32)

    return pl.pallas_call(
        functools.partial(kernel, nz, nb),
        out_shape=jax.ShapeDtypeStruct(matrix.shape, matrix.dtype),
        in_specs=[
            pl.BlockSpec(memory_space=pl.ANY),
            pl.BlockSpec(memory_space=pl.ANY),
            pl.BlockSpec(memory_space=pl.ANY),
        ],
        out_specs=pl.BlockSpec(memory_space=pltpu.VMEM),
        scratch_shapes=[
            pltpu.VMEM(pivots.shape, jnp.int32), vm(*inverses.shape), DMA((2,)),
            vm(2, nb, nb), vm(nz, 3, ch, nb), vm(2, nz, 3, ch, nb), vm(nz, 3, ch, nb), vm(2, nz, 3, ch, nb),
            vm(3, nb, nb), vm(2, nb, nb), vm(nb, nb),
            vm(nz - 1, 3, ch, nb), vm(nz - 1, 3, ch, nb),
            DMA, DMA, DMA, DMA((nz,)), DMA((2,)),
            DMA((nz - 1,)), DMA((nz - 1,)), DMA((nz - 1,)), DMA((nz - 1,)),
            DMA((nz - 1,)), DMA((nz - 1,)), DMA((nz - 1,)), DMA((nz - 1,)),
            DMA((nz,)), DMA((nz,)), DMA((nz,)), DMA((nz,)),
            DMA((2, NX)), DMA, DMA((NY,)), DMA((3,)),
            DMA((2, NX, PX)), DMA((PX,)), DMA((NY, PX)), DMA((3, PX)),
            DMA, DMA,
        ],
        compiler_params=pltpu.CompilerParams(
            collective_id=0, has_side_effects=True, vmem_limit_bytes=60 * 2**20
        ),
        name="panels",
    )(matrix, pivots, inverses)


def solution(mesh):
    placed = (P("row", "col"), P(), P())
    return jax.shard_map(
        on_device, mesh=mesh, in_specs=placed, out_specs=P("row", "col"), check_vma=False
    )
```

```python
import functools

import jax
import jax.numpy as jnp
from jax import lax
from jax.experimental import pallas as pl
from jax.experimental.pallas import tpu as pltpu
from jax.sharding import PartitionSpec as P

MESH = pl.DeviceIdType.MESH
F32 = jnp.float32
BF16 = jnp.bfloat16
NX, NY = 4, 4
RING = ((0, 1, 2, 3, 4, 5, 6, 7, 8), (0, -1, -2, -3, -4, -5, -6, -7))
RS_WAY, D_WAY, S_WAY, T_WAY = RING, RING, RING, RING
AT_D, AT_S, AT_T2, AT_T, AT_X2 = 4, 8, 9, 10, 14
RS_CUT, D_CUT, S_CUT, T_CUT = 3, 3, 1, 3
PER, PX, GAP_X = 5, 2, 2


def dot(a, b):
    return jnp.dot(a, b, preferred_element_type=F32)


def split2(a):
    hi = a.astype(BF16)
    return hi, (a - hi.astype(F32)).astype(BF16)


def split3(a):
    hi = a.astype(BF16)
    rest = a - hi.astype(F32)
    mid = rest.astype(BF16)
    return hi, mid, (rest - mid.astype(F32)).astype(BF16)


def mm(a, b):
    ah, al = split2(a)
    bh, bl = split2(b)
    return dot(ah, bh) + (dot(ah, bl) + dot(al, bh))


def select_rows(onehot, b):
    hi, mid, lo = split3(b)
    return dot(onehot, hi) + dot(onehot, mid) + dot(onehot, lo)


def kernel(
    nz, nb,
    a_ref, piv_hbm, inv_hbm, o_ref,
    piv_ref, inv_ref, sm_s,
    B, Pt, SG, DG, TG, XG, NBf, NX_, got, put,
    ld_s, ex_s, ex_r, ds_s, ds_r, rs_s, rs_r, dg_s, dg_r, sg_s, sg_r, tg_s, tg_r, ft_s, ft_r, fs_s, fs_r,
    t1_s, t1_r, t2_s, t2_r, x1_s, x1_r, x2_s, x2_r, nx_s, nx_r,
):
    row = lax.axis_index("row")
    q = lax.axis_index("col")
    z, c = row // 2, row % 2
    x, y = q // NY, q % NY
    ch = nb // nz
    up = 2 * ((z + 1) % nz) + c
    sib = 2 * z + 1 - c
    source = jnp.logical_and(jnp.logical_and(x == 0, y < 3), c == 0)

    def dev(r, k):
        return {"row": r, "col": k}

    def remote(src, dst, ss, rs, r, k):
        return pltpu.make_async_remote_copy(
            src_ref=src, dst_ref=dst, send_sem=ss, recv_sem=rs,
            device_id=dev(r, k), device_id_type=MESH,
        )

    other = pl.multiple_of((1 - c) * nb, nb)
    mine = pl.multiple_of(c * nb, nb)
    load = pltpu.make_async_copy(a_ref.at[:, pl.ds(mine, nb)], B.at[c], ld_s)
    load.start()
    load_piv = pltpu.make_async_copy(piv_hbm, piv_ref, sm_s.at[0])
    load_inv = pltpu.make_async_copy(inv_hbm, inv_ref, sm_s.at[1])
    load_piv.start()
    load_inv.start()

    bar = pltpu.get_barrier_semaphore()

    def greet(r, k):
        pl.semaphore_signal(bar, inc=1, device_id=dev(r, k), device_id_type=MESH)

    greet(sib, q)
    for d in (1, 2, nz - 1, nz - 2):
        greet(2 * ((z + d) % nz) + c, q)
    for d in range(1, NY):
        greet(row, x * NY + (y + d) % NY)

    @pl.when(z != 0)
    def _():
        greet(c, q)

    @pl.when(z != 1)
    def _():
        greet(2 + c, q)

    @pl.when(jnp.logical_and(x != 0, y < 3))
    def _():
        greet(2 * z, y)

    expected = (
        5 + (NY - 1)
        + jnp.where(z <= 1, nz - 1, 0)
        + jnp.where(source, 2 * (NX - 1), 0)
    )
    pl.semaphore_wait(bar, expected)
    swap = remote(a_ref.at[:, pl.ds(other, nb)], B.at[c], ex_s, ex_r, sib, q)
    swap.start()
    load_piv.wait()
    lane = lax.broadcasted_iota(jnp.int32, (nb, nb), 1)
    subl = lax.broadcasted_iota(jnp.int32, (nb, nb), 0)
    prow = [piv_ref[k:k + 1, :].astype(F32) for k in range(3)]
    eye = lane == subl
    pcol = [
        jnp.max(jnp.where(eye, jnp.broadcast_to(p, (nb, nb)), -1.0), axis=1, keepdims=True)
        for p in prow
    ]
    lanef = lane.astype(F32)

    def back(v, k):
        n = v.shape[0]
        hit = jnp.where(
            jnp.broadcast_to(v, (n, nb)) == jnp.broadcast_to(prow[k], (n, nb)),
            lanef[:1, :] + float(k * nb), -1.0,
        )
        best = jnp.max(hit, axis=1, keepdims=True)
        return jnp.where(best >= 0.0, best, v)

    slots = [pcol[0], back(pcol[1], 0), back(back(pcol[2], 1), 0)]
    base = (z * 2 * nb).astype(F32)
    own = [subl[:, :1].astype(F32) + base + float(h * nb) for h in range(2)]
    came = [back(back(back(g, 2), 1), 0) for g in own]
    here = lax.broadcasted_iota(jnp.int32, (nb, 2 * nb), 1).astype(F32) + base

    load.wait()
    swap.wait_recv()

    def ring(i):
        return lax.rem(i + 2 * nz, nz)

    def share(which, d):
        i = ring(z + d)
        rows = pl.ds(pl.multiple_of(i * ch, ch), ch)
        if which == 0:
            return remote(B.at[:, rows], DG.at[i, pl.ds(0, 2)], ds_s.at[d], ds_r.at[0], 2 * i + c, q)
        return remote(B.at[pl.ds(0, 1), rows], DG.at[i, pl.ds(2, 1)], ds_s.at[d], ds_r.at[1], 2 * i + c, q)

    far_first = sorted(range(1, nz), key=lambda d: -min(d, nz - d))

    @pl.when(z == 0)
    def _():
        DG[0, 0:2] = B[:, 0:ch]

    @pl.when(z == 1)
    def _():
        DG[1, 2] = B[0, ch:2 * ch]

    parts = split3(B[...].reshape(2 * nb, nb))
    for k in range(3):
        oh = (jnp.broadcast_to(slots[k], (nb, 2 * nb)) == here).astype(F32).astype(BF16)
        part = dot(oh, parts[0]) + dot(oh, parts[1]) + dot(oh, parts[2])
        Pt[:, k] = part.reshape(nz, ch, nb)

    sent = []
    def begin(cp):
        cp.start()
        sent.append(cp)
        return cp

    flight = {}

    def chip(d):
        return 2 * ring(z + d) + c

    def cuts(n):
        return [(p, pl.ds(p * (3 // n), 3 // n)) for p in range(n)]

    def rs_step(t):
        for p, ks in cuts(RS_CUT):
            for w, route in enumerate(RS_WAY):
                n = len(route) - 1
                at = sum(len(r) - 1 for r in RS_WAY[:w]) + t
                if 0 < t <= n:
                    flight.pop(("rs", w, p)).wait_recv()
                if t < n:
                    far = route[n - t]
                    i = ring(z + far)
                    put[at, ks] = Pt[i, ks] if t == 0 else Pt[i, ks] + got[at - 1, ks]
                    flight["rs", w, p] = begin(
                        remote(
                            put.at[at, ks], got.at[at, ks], rs_s.at[at, p], rs_r.at[at, p],
                            chip(far - route[n - t - 1]), q,
                        )
                    )

    def ag_step(name, way, cut, buf, t, ss, rs, forward=None):
        if t == 0 and forward is not None:
            forward(0, z)
        for p, ks in cuts(cut):
            for w, route in enumerate(way):
                n = len(route) - 1
                at = sum(len(r) - 1 for r in way[:w]) + t
                if 0 < t <= n:
                    flight.pop((name, w, p)).wait_recv()
                if t < n:
                    i = ring(z - route[t])
                    flight[name, w, p] = begin(
                        remote(
                            buf.at[i, ks], buf.at[i, ks], ss.at[at, p], rs.at[at, p],
                            chip(route[t + 1] - route[t]), q,
                        )
                    )
        for w, route in enumerate(way):
            if forward is not None and 0 < t <= len(route) - 1:
                forward(sum(len(r) - 1 for r in way[:w]) + t, z - route[t])

    tmine = TG.at[c]
    smine = SG.at[c]
    crossing = []

    def to_sibling(buf, ss, rs):
        def forward(slot, i):
            i = ring(i)
            cp = begin(remote(buf.at[i], buf.at[i], ss.at[slot], rs.at[slot], sib, q))
            crossing.append(cp)
        return forward

    def part(p):
        return pl.ds(p * (nb // PX), nb // PX)

    def strips(h):
        for p in range(PX):
            for d in range(1 - h, NX):
                yield remote(
                    NBf.at[h, part(p)], XG.at[y, part(p)], x1_s.at[h, d, p], x1_r.at[p], 2 * z + h, d * NY + y
                )

    def strips_y(d, p):
        piece = XG.at[y, part(p)]
        return remote(piece, piece, x2_s.at[d, p], x2_r.at[y, p], row, x * NY + (y + d) % NY)

    def rounds(way):
        return max(len(r) for r in way) - 1

    n_rs, n_d, n_s, n_t = rounds(RS_WAY), rounds(D_WAY), rounds(S_WAY), rounds(T_WAY)
    at_x = AT_D + n_d
    for tick in range(max(n_rs, AT_D + n_d, AT_S + n_s, AT_T + n_t, AT_X2 + GAP_X) + 1):
        if tick <= n_rs:
            rs_step(tick)
        for which in range(2):
            @pl.when(z == which)
            def _(which=which):
                for d in far_first[tick * PER:(tick + 1) * PER]:
                    share(which, d).start()

        if tick == AT_S:
            total, at = Pt[z], -1
            for route in RS_WAY:
                at += len(route) - 1
                total += got[at]
            SG[c, z] = total

            @pl.when(source)
            def _():
                first = jnp.where(y == 0, 1, 0)
                second = jnp.where(y == 2, 1, 2)
                for d in range(1, NX):
                    remote(SG.at[0, z, first], TG.at[0, z, y], t1_s.at[0, d], t1_r, 2 * z, d * NY + y).start()
                for d in range(NX):
                    remote(
                        SG.at[0, z, second], TG.at[1, z, y], t1_s.at[1, d], t1_r, 2 * z + 1, d * NY + y
                    ).start()
                TG[0, z, y] = SG[0, z, first]
        if AT_S <= tick <= AT_S + n_s:
            ag_step("s", S_WAY, S_CUT, smine, tick - AT_S, sg_s, sg_r, to_sibling(smine, fs_s, fs_r))
        if tick == AT_T2:
            @pl.when(y < 3)
            def _():
                piece = TG.at[c, z, y]

                @pl.when(jnp.logical_not(source))
                def _():
                    remote(piece, piece, t1_s.at[0, 0], t1_r, row, y).wait_recv()

                for d in range(1, NY):
                    remote(piece, piece, t2_s.at[d], t2_r.at[y], row, x * NY + (y + d) % NY).start()

        if tick == AT_D:
            @pl.when(z != 0)
            def _():
                remote(B.at[:, 0:ch], DG.at[z, pl.ds(0, 2)], ds_s.at[0], ds_r.at[0], up, q).wait_recv()

            @pl.when(z != 1)
            def _():
                remote(
                    B.at[pl.ds(0, 1), 0:ch], DG.at[z, pl.ds(2, 1)], ds_s.at[0], ds_r.at[1], up, q
                ).wait_recv()
        if AT_D <= tick <= AT_D + n_d:
            ag_step("d", D_WAY, D_CUT, DG, tick - AT_D, dg_s, dg_r)
        if tick == AT_T:
            for j in range(3):
                @pl.when(y != j)
                def _(j=j):
                    piece = TG.at[c, z, j]
                    remote(piece, piece, t2_s.at[0], t2_r.at[j], row, q).wait_recv()
        if AT_T <= tick <= AT_T + n_t:
            ag_step("t", T_WAY, T_CUT, tmine, tick - AT_T, tg_s, tg_r, to_sibling(tmine, ft_s, ft_r))
        if tick == at_x:
            dg = [split3(DG[:, k].reshape(nb, nb)) for k in range(3)]
            for h in range(2):
                moved = jnp.zeros((nb, nb), F32)
                for k in range(3):
                    oh = jnp.broadcast_to(came[h], (nb, nb)) == lanef + float(k * nb)
                    oh = oh.astype(F32).astype(BF16)
                    moved += dot(oh, dg[k][0]) + dot(oh, dg[k][1]) + dot(oh, dg[k][2])
                keep = jnp.broadcast_to(came[h], (nb, nb)) == jnp.broadcast_to(own[h], (nb, nb))
                NBf[h] = jnp.where(keep, B[h], moved)

                @pl.when(source)
                def _(h=h):
                    for cp in strips(h):
                        cp.start()
                    if h == 0:
                        XG[y] = NBf[0]

            crossing.append(begin(remote(NBf.at[1 - c], NX_, nx_s, nx_r, sib, q)))
        for p in range(PX):
            if tick == AT_X2 + p * GAP_X // PX:
                @pl.when(y < 3)
                def _(p=p):
                    piece = XG.at[y, part(p)]

                    @pl.when(jnp.logical_not(source))
                    def _():
                        remote(piece, piece, x1_s.at[0, 0, p], x1_r.at[p], row, y).wait_recv()

                    for d in range(1, NY):
                        strips_y(d, p).start()

    for cp in crossing:
        cp.wait_recv()

    load_inv.wait()
    i0, i1, i2 = inv_ref[0], inv_ref[1], inv_ref[2]
    t10, t01, t02, t20, t21, t12 = (TG[j // 3, :, j % 3].reshape(nb, nb) for j in range(6))
    l10, l20 = mm(t10, i0), mm(t20, i0)
    l21 = mm(t21 - mm(l20, t01), i1)
    u12 = t12 - mm(l10, t02)
    us = []
    for h in range(2):
        s0, s1, s2 = (SG[h, :, k].reshape(nb, nb) for k in range(3))
        u1 = s1 - mm(l10, s0)
        us.append((s0, u1, s2 - mm(l20, s0) - mm(l21, u1)))

    for j in range(3):
        @pl.when(y != j)
        def _(j=j):
            for p in range(PX):
                piece = XG.at[j, part(p)]
                remote(piece, piece, x2_s.at[0, p], x2_r.at[j, p], row, q).wait_recv()
    l0 = mm(XG[0], i0)
    l1 = mm(XG[1] - mm(l0, t01), i1)
    l2 = mm(XG[2] - mm(l0, t02) - mm(l1, u12), i2)
    for h in range(2):
        cols = pl.ds(h * nb, nb)
        u0, u1, u2 = us[h]

        @pl.when(row >= 3)
        def _(h=h, cols=cols, u0=u0, u1=u1, u2=u2):
            @pl.when(c == h)
            def _():
                o_ref[:, cols] = NBf[h]

            @pl.when(c != h)
            def _():
                o_ref[:, cols] = NX_[...]

            o_ref[:, cols] -= mm(l0, u0) + mm(l1, u1) + mm(l2, u2)

        for r, u in enumerate((u0, u1, u2)):
            @pl.when(row == r)
            def _(cols=cols, u=u):
                o_ref[:, cols] = u
    for k, l in enumerate((l0, l1, l2)):
        @pl.when(jnp.logical_and(row >= 3, q == k))
        def _(l=l):
            o_ref[:, 0:nb] = l
    for r, k, l in ((1, 0, l10), (2, 0, l20), (2, 1, l21)):
        @pl.when(jnp.logical_and(row == r, q == k))
        def _(l=l):
            o_ref[:, 0:nb] = l

    swap.wait_send()
    for cp in sent:
        cp.wait_send()
    for which in range(2):
        @pl.when(z == which)
        def _(which=which):
            for d in range(1, nz):
                share(which, d).wait_send()

    @pl.when(source)
    def _():
        for d in range(1, NX):
            remote(SG.at[0, z, 0], TG.at[0, z, y], t1_s.at[0, d], t1_r, 2 * z, d * NY + y).wait_send()
        for d in range(NX):
            remote(SG.at[0, z, 0], TG.at[1, z, y], t1_s.at[1, d], t1_r, 2 * z + 1, d * NY + y).wait_send()
        for h in range(2):
            for cp in strips(h):
                cp.wait_send()

    @pl.when(y < 3)
    def _():
        for d in range(1, NY):
            to = x * NY + (y + d) % NY
            piece = TG.at[c, z, y]
            remote(piece, piece, t2_s.at[d], t2_r.at[y], row, to).wait_send()
            for p in range(PX):
                strips_y(d, p).wait_send()


def on_device(matrix, pivots, inverses):
    nb = inverses.shape[1]
    nz = lax.axis_size("row") // 2
    ch = nb // nz
    DMA = pltpu.SemaphoreType.DMA

    def vm(*shape):
        return pltpu.VMEM(shape, F32)

    return pl.pallas_call(
        functools.partial(kernel, nz, nb),
        out_shape=jax.ShapeDtypeStruct(matrix.shape, matrix.dtype),
        in_specs=[
            pl.BlockSpec(memory_space=pl.ANY),
            pl.BlockSpec(memory_space=pl.ANY),
            pl.BlockSpec(memory_space=pl.ANY),
        ],
        out_specs=pl.BlockSpec(memory_space=pltpu.VMEM),
        scratch_shapes=[
            pltpu.VMEM(pivots.shape, jnp.int32), vm(*inverses.shape), DMA((2,)),
            vm(2, nb, nb), vm(nz, 3, ch, nb), vm(2, nz, 3, ch, nb), vm(nz, 3, ch, nb), vm(2, nz, 3, ch, nb),
            vm(3, nb, nb), vm(2, nb, nb), vm(nb, nb),
            vm(nz - 1, 3, ch, nb), vm(nz - 1, 3, ch, nb),
            DMA, DMA, DMA, DMA((nz,)), DMA((2,)),
            DMA((nz - 1, 3)), DMA((nz - 1, 3)), DMA((nz - 1, 3)), DMA((nz - 1, 3)),
            DMA((nz - 1, 3)), DMA((nz - 1, 3)), DMA((nz - 1, 3)), DMA((nz - 1, 3)),
            DMA((nz,)), DMA((nz,)), DMA((nz,)), DMA((nz,)),
            DMA((2, NX)), DMA, DMA((NY,)), DMA((3,)),
            DMA((2, NX, PX)), DMA((PX,)), DMA((NY, PX)), DMA((3, PX)),
            DMA, DMA,
        ],
        compiler_params=pltpu.CompilerParams(
            collective_id=0, has_side_effects=True, vmem_limit_bytes=60 * 2**20
        ),
        name="panels",
    )(matrix, pivots, inverses)


def solution(mesh):
    placed = (P("row", "col"), P(), P())
    return jax.shard_map(
        on_device, mesh=mesh, in_specs=placed, out_specs=P("row", "col"), check_vma=False
    )
```

```python
import functools

import jax
import jax.numpy as jnp
from jax import lax
from jax.experimental import pallas as pl
from jax.experimental.pallas import tpu as pltpu
from jax.sharding import PartitionSpec as P

MESH = pl.DeviceIdType.MESH
F32 = jnp.float32
BF16 = jnp.bfloat16
NX, NY = 4, 4
RING = ((0, 1, 2, 3, 4, 5, 6, 7, 8), (0, -1, -2, -3, -4, -5, -6, -7))
RS_WAY, D_WAY, S_WAY, T_WAY = RING, RING, RING, RING
AT_D, AT_S, AT_T2, AT_T, AT_X2 = 4, 8, 9, 10, 14
RS_CUT, D_CUT, S_CUT, T_CUT = 3, 3, 1, 3
PER, PX, GAP_X = 5, 2, 2


def dot(a, b):
    return jnp.dot(a, b, preferred_element_type=F32)


def split2(a):
    hi = a.astype(BF16)
    return hi, (a - hi.astype(F32)).astype(BF16)


def split3(a):
    hi = a.astype(BF16)
    rest = a - hi.astype(F32)
    mid = rest.astype(BF16)
    return hi, mid, (rest - mid.astype(F32)).astype(BF16)


def mm(a, b):
    ah, al = split2(a)
    bh, bl = split2(b)
    return dot(ah, bh) + (dot(ah, bl) + dot(al, bh))


def select_rows(onehot, b):
    hi, mid, lo = split3(b)
    return dot(onehot, hi) + dot(onehot, mid) + dot(onehot, lo)


def kernel(
    nz, nb,
    a_ref, piv_hbm, inv_hbm, o_ref,
    piv_ref, inv_ref, sm_s,
    B, Pt, SG, DG, TG, XG, NBf, NX_, got, put,
    ld_s, ex_s, ex_r, ds_s, ds_r, rs_s, rs_r, dg_s, dg_r, sg_s, sg_r, tg_s, tg_r, ft_s, ft_r, fs_s, fs_r,
    t1_s, t1_r, t2_s, t2_r, x1_s, x1_r, x2_s, x2_r, nx_s, nx_r,
):
    row = lax.axis_index("row")
    q = lax.axis_index("col")
    z, c = row // 2, row % 2
    x, y = q // NY, q % NY
    ch = nb // nz
    up = 2 * ((z + 1) % nz) + c
    sib = 2 * z + 1 - c
    source = jnp.logical_and(jnp.logical_and(x == 0, y < 3), c == 0)

    def dev(r, k):
        return {"row": r, "col": k}

    def remote(src, dst, ss, rs, r, k):
        return pltpu.make_async_remote_copy(
            src_ref=src, dst_ref=dst, send_sem=ss, recv_sem=rs,
            device_id=dev(r, k), device_id_type=MESH,
        )

    other = pl.multiple_of((1 - c) * nb, nb)
    mine = pl.multiple_of(c * nb, nb)
    load = pltpu.make_async_copy(a_ref.at[:, pl.ds(mine, nb)], B.at[c], ld_s)
    load.start()
    load_piv = pltpu.make_async_copy(piv_hbm, piv_ref, sm_s.at[0])
    load_inv = pltpu.make_async_copy(inv_hbm, inv_ref, sm_s.at[1])
    load_piv.start()
    load_inv.start()

    bar = pltpu.get_barrier_semaphore()

    def greet(r, k):
        pl.semaphore_signal(bar, inc=1, device_id=dev(r, k), device_id_type=MESH)

    greet(sib, q)
    for d in (1, 2, nz - 1, nz - 2):
        greet(2 * ((z + d) % nz) + c, q)
    for d in range(1, NY):
        greet(row, x * NY + (y + d) % NY)

    @pl.when(z != 0)
    def _():
        greet(c, q)

    @pl.when(z != 1)
    def _():
        greet(2 + c, q)

    @pl.when(jnp.logical_and(x != 0, y < 3))
    def _():
        greet(2 * z, y)

    expected = (
        5 + (NY - 1)
        + jnp.where(z <= 1, nz - 1, 0)
        + jnp.where(source, 2 * (NX - 1), 0)
    )
    pl.semaphore_wait(bar, expected)
    swap = remote(a_ref.at[:, pl.ds(other, nb)], B.at[c], ex_s, ex_r, sib, q)
    swap.start()
    load_piv.wait()
    lane = lax.broadcasted_iota(jnp.int32, (nb, nb), 1)
    subl = lax.broadcasted_iota(jnp.int32, (nb, nb), 0)
    prow = [piv_ref[k:k + 1, :].astype(F32) for k in range(3)]
    eye = lane == subl
    pcol = [
        jnp.max(jnp.where(eye, jnp.broadcast_to(p, (nb, nb)), -1.0), axis=1, keepdims=True)
        for p in prow
    ]
    lanef = lane.astype(F32)

    def back(v, k):
        n = v.shape[0]
        hit = jnp.where(
            jnp.broadcast_to(v, (n, nb)) == jnp.broadcast_to(prow[k], (n, nb)),
            lanef[:1, :] + float(k * nb), -1.0,
        )
        best = jnp.max(hit, axis=1, keepdims=True)
        return jnp.where(best >= 0.0, best, v)

    slots = [pcol[0], back(pcol[1], 0), back(back(pcol[2], 1), 0)]
    base = (z * 2 * nb).astype(F32)
    own = [subl[:, :1].astype(F32) + base + float(h * nb) for h in range(2)]
    came = [back(back(back(g, 2), 1), 0) for g in own]
    here = lax.broadcasted_iota(jnp.int32, (nb, 2 * nb), 1).astype(F32) + base

    load.wait()
    swap.wait_recv()

    def ring(i):
        return lax.rem(i + 2 * nz, nz)

    def share(which, d):
        i = ring(z + d)
        rows = pl.ds(pl.multiple_of(i * ch, ch), ch)
        if which == 0:
            return remote(B.at[:, rows], DG.at[i, pl.ds(0, 2)], ds_s.at[d], ds_r.at[0], 2 * i + c, q)
        return remote(B.at[pl.ds(0, 1), rows], DG.at[i, pl.ds(2, 1)], ds_s.at[d], ds_r.at[1], 2 * i + c, q)

    far_first = sorted(range(1, nz), key=lambda d: -min(d, nz - d))

    @pl.when(z == 0)
    def _():
        DG[0, 0:2] = B[:, 0:ch]

    @pl.when(z == 1)
    def _():
        DG[1, 2] = B[0, ch:2 * ch]

    parts = split3(B[...].reshape(2 * nb, nb))
    for k in range(3):
        oh = (jnp.broadcast_to(slots[k], (nb, 2 * nb)) == here).astype(F32).astype(BF16)
        part = dot(oh, parts[0]) + dot(oh, parts[1]) + dot(oh, parts[2])
        Pt[:, k] = part.reshape(nz, ch, nb)

    sent = []
    def begin(cp):
        cp.start()
        sent.append(cp)
        return cp

    flight = {}

    def chip(d):
        return 2 * ring(z + d) + c

    def cuts(n):
        return [(p, pl.ds(p * (3 // n), 3 // n)) for p in range(n)]

    def rs_step(t):
        for p, ks in cuts(RS_CUT):
            for w, route in enumerate(RS_WAY):
                n = len(route) - 1
                at = sum(len(r) - 1 for r in RS_WAY[:w]) + t
                if 0 < t <= n:
                    flight.pop(("rs", w, p)).wait_recv()
                if t < n:
                    far = route[n - t]
                    i = ring(z + far)
                    put[at, ks] = Pt[i, ks] if t == 0 else Pt[i, ks] + got[at - 1, ks]
                    flight["rs", w, p] = begin(
                        remote(
                            put.at[at, ks], got.at[at, ks], rs_s.at[at, p], rs_r.at[at, p],
                            chip(far - route[n - t - 1]), q,
                        )
                    )

    def ag_step(name, way, cut, buf, t, ss, rs, forward=None):
        if t == 0 and forward is not None:
            forward(0, z)
        for p, ks in cuts(cut):
            for w, route in enumerate(way):
                n = len(route) - 1
                at = sum(len(r) - 1 for r in way[:w]) + t
                if 0 < t <= n:
                    flight.pop((name, w, p)).wait_recv()
                if t < n:
                    i = ring(z - route[t])
                    flight[name, w, p] = begin(
                        remote(
                            buf.at[i, ks], buf.at[i, ks], ss.at[at, p], rs.at[at, p],
                            chip(route[t + 1] - route[t]), q,
                        )
                    )
        for w, route in enumerate(way):
            if forward is not None and 0 < t <= len(route) - 1:
                forward(sum(len(r) - 1 for r in way[:w]) + t, z - route[t])

    tmine = TG.at[c]
    smine = SG.at[c]
    crossing = []

    def to_sibling(buf, ss, rs):
        def forward(slot, i):
            i = ring(i)
            cp = begin(remote(buf.at[i], buf.at[i], ss.at[slot], rs.at[slot], sib, q))
            crossing.append(cp)
        return forward

    def part(p):
        return pl.ds(p * (nb // PX), nb // PX)

    def strips(h):
        for p in range(PX):
            for d in range(1 - h, NX):
                yield remote(
                    NBf.at[h, part(p)], XG.at[y, part(p)], x1_s.at[h, d, p], x1_r.at[p], 2 * z + h, d * NY + y
                )

    def strips_y(d, p):
        piece = XG.at[y, part(p)]
        return remote(piece, piece, x2_s.at[d, p], x2_r.at[y, p], row, x * NY + (y + d) % NY)

    def rounds(way):
        return max(len(r) for r in way) - 1

    n_rs, n_d, n_s, n_t = rounds(RS_WAY), rounds(D_WAY), rounds(S_WAY), rounds(T_WAY)
    at_x = AT_D + n_d
    for tick in range(max(n_rs, AT_D + n_d, AT_S + n_s, AT_T + n_t, AT_X2 + GAP_X) + 1):
        if tick <= n_rs:
            rs_step(tick)
        for which in range(2):
            @pl.when(z == which)
            def _(which=which):
                for d in far_first[tick * PER:(tick + 1) * PER]:
                    share(which, d).start()

        if tick == AT_S:
            total, at = Pt[z], -1
            for route in RS_WAY:
                at += len(route) - 1
                total += got[at]
            SG[c, z] = total

            @pl.when(source)
            def _():
                first = jnp.where(y == 0, 1, 0)
                second = jnp.where(y == 2, 1, 2)
                for d in range(1, NX):
                    remote(SG.at[0, z, first], TG.at[0, z, y], t1_s.at[0, d], t1_r, 2 * z, d * NY + y).start()
                for d in range(NX):
                    remote(
                        SG.at[0, z, second], TG.at[1, z, y], t1_s.at[1, d], t1_r, 2 * z + 1, d * NY + y
                    ).start()
                TG[0, z, y] = SG[0, z, first]
        if tick == AT_T2:
            @pl.when(y < 3)
            def _():
                piece = TG.at[c, z, y]

                @pl.when(jnp.logical_not(source))
                def _():
                    remote(piece, piece, t1_s.at[0, 0], t1_r, row, y).wait_recv()

                for d in range(1, NY):
                    remote(piece, piece, t2_s.at[d], t2_r.at[y], row, x * NY + (y + d) % NY).start()

        if tick == AT_T:
            for j in range(3):
                @pl.when(y != j)
                def _(j=j):
                    piece = TG.at[c, z, j]
                    remote(piece, piece, t2_s.at[0], t2_r.at[j], row, q).wait_recv()
        if AT_T <= tick <= AT_T + n_t:
            ag_step("t", T_WAY, T_CUT, tmine, tick - AT_T, tg_s, tg_r, to_sibling(tmine, ft_s, ft_r))
        if AT_S <= tick <= AT_S + n_s:
            ag_step("s", S_WAY, S_CUT, smine, tick - AT_S, sg_s, sg_r, to_sibling(smine, fs_s, fs_r))
        if tick == AT_D:
            @pl.when(z != 0)
            def _():
                remote(B.at[:, 0:ch], DG.at[z, pl.ds(0, 2)], ds_s.at[0], ds_r.at[0], up, q).wait_recv()

            @pl.when(z != 1)
            def _():
                remote(
                    B.at[pl.ds(0, 1), 0:ch], DG.at[z, pl.ds(2, 1)], ds_s.at[0], ds_r.at[1], up, q
                ).wait_recv()
        if AT_D <= tick <= AT_D + n_d:
            ag_step("d", D_WAY, D_CUT, DG, tick - AT_D, dg_s, dg_r)
        if tick == at_x:
            dg = [split3(DG[:, k].reshape(nb, nb)) for k in range(3)]
            for h in range(2):
                moved = jnp.zeros((nb, nb), F32)
                for k in range(3):
                    oh = jnp.broadcast_to(came[h], (nb, nb)) == lanef + float(k * nb)
                    oh = oh.astype(F32).astype(BF16)
                    moved += dot(oh, dg[k][0]) + dot(oh, dg[k][1]) + dot(oh, dg[k][2])
                keep = jnp.broadcast_to(came[h], (nb, nb)) == jnp.broadcast_to(own[h], (nb, nb))
                NBf[h] = jnp.where(keep, B[h], moved)

                @pl.when(source)
                def _(h=h):
                    for cp in strips(h):
                        cp.start()
                    if h == 0:
                        XG[y] = NBf[0]

            crossing.append(begin(remote(NBf.at[1 - c], NX_, nx_s, nx_r, sib, q)))
        for p in range(PX):
            if tick == AT_X2 + p * GAP_X // PX:
                @pl.when(y < 3)
                def _(p=p):
                    piece = XG.at[y, part(p)]

                    @pl.when(jnp.logical_not(source))
                    def _():
                        remote(piece, piece, x1_s.at[0, 0, p], x1_r.at[p], row, y).wait_recv()

                    for d in range(1, NY):
                        strips_y(d, p).start()

    for cp in crossing:
        cp.wait_recv()

    load_inv.wait()
    i0, i1, i2 = inv_ref[0], inv_ref[1], inv_ref[2]
    t10, t01, t02, t20, t21, t12 = (TG[j // 3, :, j % 3].reshape(nb, nb) for j in range(6))
    l10, l20 = mm(t10, i0), mm(t20, i0)
    l21 = mm(t21 - mm(l20, t01), i1)
    u12 = t12 - mm(l10, t02)
    us = []
    for h in range(2):
        s0, s1, s2 = (SG[h, :, k].reshape(nb, nb) for k in range(3))
        u1 = s1 - mm(l10, s0)
        us.append((s0, u1, s2 - mm(l20, s0) - mm(l21, u1)))

    for j in range(3):
        @pl.when(y != j)
        def _(j=j):
            for p in range(PX):
                piece = XG.at[j, part(p)]
                remote(piece, piece, x2_s.at[0, p], x2_r.at[j, p], row, q).wait_recv()
    l0 = mm(XG[0], i0)
    l1 = mm(XG[1] - mm(l0, t01), i1)
    l2 = mm(XG[2] - mm(l0, t02) - mm(l1, u12), i2)
    for h in range(2):
        cols = pl.ds(h * nb, nb)
        u0, u1, u2 = us[h]

        @pl.when(row >= 3)
        def _(h=h, cols=cols, u0=u0, u1=u1, u2=u2):
            @pl.when(c == h)
            def _():
                o_ref[:, cols] = NBf[h]

            @pl.when(c != h)
            def _():
                o_ref[:, cols] = NX_[...]

            o_ref[:, cols] -= mm(l0, u0) + mm(l1, u1) + mm(l2, u2)

        for r, u in enumerate((u0, u1, u2)):
            @pl.when(row == r)
            def _(cols=cols, u=u):
                o_ref[:, cols] = u
    for k, l in enumerate((l0, l1, l2)):
        @pl.when(jnp.logical_and(row >= 3, q == k))
        def _(l=l):
            o_ref[:, 0:nb] = l
    for r, k, l in ((1, 0, l10), (2, 0, l20), (2, 1, l21)):
        @pl.when(jnp.logical_and(row == r, q == k))
        def _(l=l):
            o_ref[:, 0:nb] = l

    swap.wait_send()
    for cp in sent:
        cp.wait_send()
    for which in range(2):
        @pl.when(z == which)
        def _(which=which):
            for d in range(1, nz):
                share(which, d).wait_send()

    @pl.when(source)
    def _():
        for d in range(1, NX):
            remote(SG.at[0, z, 0], TG.at[0, z, y], t1_s.at[0, d], t1_r, 2 * z, d * NY + y).wait_send()
        for d in range(NX):
            remote(SG.at[0, z, 0], TG.at[1, z, y], t1_s.at[1, d], t1_r, 2 * z + 1, d * NY + y).wait_send()
        for h in range(2):
            for cp in strips(h):
                cp.wait_send()

    @pl.when(y < 3)
    def _():
        for d in range(1, NY):
            to = x * NY + (y + d) % NY
            piece = TG.at[c, z, y]
            remote(piece, piece, t2_s.at[d], t2_r.at[y], row, to).wait_send()
            for p in range(PX):
                strips_y(d, p).wait_send()


def on_device(matrix, pivots, inverses):
    nb = inverses.shape[1]
    nz = lax.axis_size("row") // 2
    ch = nb // nz
    DMA = pltpu.SemaphoreType.DMA

    def vm(*shape):
        return pltpu.VMEM(shape, F32)

    return pl.pallas_call(
        functools.partial(kernel, nz, nb),
        out_shape=jax.ShapeDtypeStruct(matrix.shape, matrix.dtype),
        in_specs=[
            pl.BlockSpec(memory_space=pl.ANY),
            pl.BlockSpec(memory_space=pl.ANY),
            pl.BlockSpec(memory_space=pl.ANY),
        ],
        out_specs=pl.BlockSpec(memory_space=pltpu.VMEM),
        scratch_shapes=[
            pltpu.VMEM(pivots.shape, jnp.int32), vm(*inverses.shape), DMA((2,)),
            vm(2, nb, nb), vm(nz, 3, ch, nb), vm(2, nz, 3, ch, nb), vm(nz, 3, ch, nb), vm(2, nz, 3, ch, nb),
            vm(3, nb, nb), vm(2, nb, nb), vm(nb, nb),
            vm(nz - 1, 3, ch, nb), vm(nz - 1, 3, ch, nb),
            DMA, DMA, DMA, DMA((nz,)), DMA((2,)),
            DMA((nz - 1, 3)), DMA((nz - 1, 3)), DMA((nz - 1, 3)), DMA((nz - 1, 3)),
            DMA((nz - 1, 3)), DMA((nz - 1, 3)), DMA((nz - 1, 3)), DMA((nz - 1, 3)),
            DMA((nz,)), DMA((nz,)), DMA((nz,)), DMA((nz,)),
            DMA((2, NX)), DMA, DMA((NY,)), DMA((3,)),
            DMA((2, NX, PX)), DMA((PX,)), DMA((NY, PX)), DMA((3, PX)),
            DMA, DMA,
        ],
        compiler_params=pltpu.CompilerParams(
            collective_id=0, has_side_effects=True, vmem_limit_bytes=60 * 2**20
        ),
        name="panels",
    )(matrix, pivots, inverses)


def solution(mesh):
    placed = (P("row", "col"), P(), P())
    return jax.shard_map(
        on_device, mesh=mesh, in_specs=placed, out_specs=P("row", "col"), check_vma=False
    )
```

```python
import functools

import jax
import jax.numpy as jnp
from jax import lax
from jax.experimental import pallas as pl
from jax.experimental.pallas import tpu as pltpu
from jax.sharding import PartitionSpec as P

MESH = pl.DeviceIdType.MESH
F32 = jnp.float32
BF16 = jnp.bfloat16
NX, NY = 4, 4
RING = ((0, 1, 2, 3, 4, 5, 6, 7, 8), (0, -1, -2, -3, -4, -5, -6, -7))
RS_WAY, D_WAY, S_WAY, T_WAY = RING, RING, RING, RING
AT_D, AT_S, AT_T2, AT_T, AT_X2 = 4, 8, 9, 10, 14
RS_CUT, D_CUT, S_CUT, T_CUT = 3, 3, 1, 3
PER, PX, GAP_X = 5, 2, 2


def dot(a, b):
    return jnp.dot(a, b, preferred_element_type=F32)


def split2(a):
    hi = a.astype(BF16)
    return hi, (a - hi.astype(F32)).astype(BF16)


def split3(a):
    hi = a.astype(BF16)
    rest = a - hi.astype(F32)
    mid = rest.astype(BF16)
    return hi, mid, (rest - mid.astype(F32)).astype(BF16)


def mm(a, b):
    ah, al = split2(a)
    bh, bl = split2(b)
    return dot(ah, bh) + (dot(ah, bl) + dot(al, bh))


def select_rows(onehot, b):
    hi, mid, lo = split3(b)
    return dot(onehot, hi) + dot(onehot, mid) + dot(onehot, lo)


def kernel(
    nz, nb,
    a_ref, piv_hbm, inv_hbm, o_ref,
    piv_ref, inv_ref, sm_s,
    B, Pt, SG, DG, TG, XG, NBf, NX_, got, put,
    ld_s, ex_s, ex_r, ds_s, ds_r, rs_s, rs_r, dg_s, dg_r, sg_s, sg_r, tg_s, tg_r, ft_s, ft_r, fs_s, fs_r,
    t1_s, t1_r, t2_s, t2_r, x1_s, x1_r, x2_s, x2_r, nx_s, nx_r,
):
    row = lax.axis_index("row")
    q = lax.axis_index("col")
    z, c = row // 2, row % 2
    x, y = q // NY, q % NY
    ch = nb // nz
    up = 2 * ((z + 1) % nz) + c
    sib = 2 * z + 1 - c
    source = jnp.logical_and(jnp.logical_and(x == 0, y < 3), c == 0)

    def dev(r, k):
        return {"row": r, "col": k}

    def remote(src, dst, ss, rs, r, k):
        return pltpu.make_async_remote_copy(
            src_ref=src, dst_ref=dst, send_sem=ss, recv_sem=rs,
            device_id=dev(r, k), device_id_type=MESH,
        )

    other = pl.multiple_of((1 - c) * nb, nb)
    mine = pl.multiple_of(c * nb, nb)
    load = pltpu.make_async_copy(a_ref.at[:, pl.ds(mine, nb)], B.at[c], ld_s)
    load.start()
    load_piv = pltpu.make_async_copy(piv_hbm, piv_ref, sm_s.at[0])
    load_inv = pltpu.make_async_copy(inv_hbm, inv_ref, sm_s.at[1])
    load_piv.start()
    load_inv.start()

    bar = pltpu.get_barrier_semaphore()

    def greet(r, k):
        pl.semaphore_signal(bar, inc=1, device_id=dev(r, k), device_id_type=MESH)

    greet(sib, q)
    for d in (1, 2, nz - 1, nz - 2):
        greet(2 * ((z + d) % nz) + c, q)
    for d in range(1, NY):
        greet(row, x * NY + (y + d) % NY)

    @pl.when(z != 0)
    def _():
        greet(c, q)

    @pl.when(z != 1)
    def _():
        greet(2 + c, q)

    @pl.when(jnp.logical_and(x != 0, y < 3))
    def _():
        greet(2 * z, y)

    expected = (
        5 + (NY - 1)
        + jnp.where(z <= 1, nz - 1, 0)
        + jnp.where(source, 2 * (NX - 1), 0)
    )
    pl.semaphore_wait(bar, expected)
    swap = remote(a_ref.at[:, pl.ds(other, nb)], B.at[c], ex_s, ex_r, sib, q)
    swap.start()
    load_piv.wait()
    lane = lax.broadcasted_iota(jnp.int32, (nb, nb), 1)
    subl = lax.broadcasted_iota(jnp.int32, (nb, nb), 0)
    prow = [piv_ref[k:k + 1, :].astype(F32) for k in range(3)]
    eye = lane == subl
    pcol = [
        jnp.max(jnp.where(eye, jnp.broadcast_to(p, (nb, nb)), -1.0), axis=1, keepdims=True)
        for p in prow
    ]
    lanef = lane.astype(F32)

    def back(v, k):
        n = v.shape[0]
        hit = jnp.where(
            jnp.broadcast_to(v, (n, nb)) == jnp.broadcast_to(prow[k], (n, nb)),
            lanef[:1, :] + float(k * nb), -1.0,
        )
        best = jnp.max(hit, axis=1, keepdims=True)
        return jnp.where(best >= 0.0, best, v)

    slots = [pcol[0], back(pcol[1], 0), back(back(pcol[2], 1), 0)]
    base = (z * 2 * nb).astype(F32)
    own = [subl[:, :1].astype(F32) + base + float(h * nb) for h in range(2)]
    came = [back(back(back(g, 2), 1), 0) for g in own]
    here = lax.broadcasted_iota(jnp.int32, (nb, 2 * nb), 1).astype(F32) + base

    load.wait()
    swap.wait_recv()

    def ring(i):
        return lax.rem(i + 2 * nz, nz)

    def share(which, d):
        i = ring(z + d)
        rows = pl.ds(pl.multiple_of(i * ch, ch), ch)
        if which == 0:
            return remote(B.at[:, rows], DG.at[i, pl.ds(0, 2)], ds_s.at[d], ds_r.at[0], 2 * i + c, q)
        return remote(B.at[pl.ds(0, 1), rows], DG.at[i, pl.ds(2, 1)], ds_s.at[d], ds_r.at[1], 2 * i + c, q)

    far_first = sorted(range(1, nz), key=lambda d: -min(d, nz - d))

    @pl.when(z == 0)
    def _():
        DG[0, 0:2] = B[:, 0:ch]

    @pl.when(z == 1)
    def _():
        DG[1, 2] = B[0, ch:2 * ch]

    parts = split3(B[...].reshape(2 * nb, nb))
    for k in range(3):
        oh = (jnp.broadcast_to(slots[k], (nb, 2 * nb)) == here).astype(F32).astype(BF16)
        part = dot(oh, parts[0]) + dot(oh, parts[1]) + dot(oh, parts[2])
        Pt[:, k] = part.reshape(nz, ch, nb)

    sent = []
    def begin(cp):
        cp.start()
        sent.append(cp)
        return cp

    flight = {}

    def chip(d):
        return 2 * ring(z + d) + c

    def cuts(n):
        return [(p, pl.ds(p * (3 // n), 3 // n)) for p in range(n)]

    def rs_step(t):
        for p, ks in cuts(RS_CUT):
            for w, route in enumerate(RS_WAY):
                n = len(route) - 1
                at = sum(len(r) - 1 for r in RS_WAY[:w]) + t
                if 0 < t <= n:
                    flight.pop(("rs", w, p)).wait_recv()
                if t < n:
                    far = route[n - t]
                    i = ring(z + far)
                    put[at, ks] = Pt[i, ks] if t == 0 else Pt[i, ks] + got[at - 1, ks]
                    flight["rs", w, p] = begin(
                        remote(
                            put.at[at, ks], got.at[at, ks], rs_s.at[at, p], rs_r.at[at, p],
                            chip(far - route[n - t - 1]), q,
                        )
                    )

    def ag_step(name, way, cut, buf, t, ss, rs, forward=None):
        if t == 0 and forward is not None:
            forward(0, z)
        for p, ks in cuts(cut):
            for w, route in enumerate(way):
                n = len(route) - 1
                at = sum(len(r) - 1 for r in way[:w]) + t
                if 0 < t <= n:
                    flight.pop((name, w, p)).wait_recv()
                if t < n:
                    i = ring(z - route[t])
                    flight[name, w, p] = begin(
                        remote(
                            buf.at[i, ks], buf.at[i, ks], ss.at[at, p], rs.at[at, p],
                            chip(route[t + 1] - route[t]), q,
                        )
                    )
        for w, route in enumerate(way):
            if forward is not None and 0 < t <= len(route) - 1:
                forward(sum(len(r) - 1 for r in way[:w]) + t, z - route[t])

    tmine = TG.at[c]
    smine = SG.at[c]
    crossing = []

    def to_sibling(buf, ss, rs):
        def forward(slot, i):
            i = ring(i)
            cp = begin(remote(buf.at[i], buf.at[i], ss.at[slot], rs.at[slot], sib, q))
            crossing.append(cp)
        return forward

    def part(p):
        return pl.ds(p * (nb // PX), nb // PX)

    def strips(h):
        for p in range(PX):
            for d in range(1 - h, NX):
                yield remote(
                    NBf.at[h, part(p)], XG.at[y, part(p)], x1_s.at[h, d, p], x1_r.at[p], 2 * z + h, d * NY + y
                )

    def strips_y(d, p):
        piece = XG.at[y, part(p)]
        return remote(piece, piece, x2_s.at[d, p], x2_r.at[y, p], row, x * NY + (y + d) % NY)

    def rounds(way):
        return max(len(r) for r in way) - 1

    n_rs, n_d, n_s, n_t = rounds(RS_WAY), rounds(D_WAY), rounds(S_WAY), rounds(T_WAY)
    at_x = AT_D + n_d
    for tick in range(max(n_rs, AT_D + n_d, AT_S + n_s, AT_T + n_t, AT_X2 + GAP_X) + 1):
        if tick <= n_rs:
            rs_step(tick)
        for which in range(2):
            @pl.when(z == which)
            def _(which=which):
                for d in far_first[tick * PER:(tick + 1) * PER]:
                    share(which, d).start()

        if tick == AT_S:
            total, at = Pt[z], -1
            for route in RS_WAY:
                at += len(route) - 1
                total += got[at]
            SG[c, z] = total

            @pl.when(source)
            def _():
                first = jnp.where(y == 0, 1, 0)
                second = jnp.where(y == 2, 1, 2)
                for d in range(1, NX):
                    remote(SG.at[0, z, first], TG.at[0, z, y], t1_s.at[0, d], t1_r, 2 * z, d * NY + y).start()
                for d in range(NX):
                    remote(
                        SG.at[0, z, second], TG.at[1, z, y], t1_s.at[1, d], t1_r, 2 * z + 1, d * NY + y
                    ).start()
                TG[0, z, y] = SG[0, z, first]
        if tick == AT_T2:
            @pl.when(y < 3)
            def _():
                piece = TG.at[c, z, y]

                @pl.when(jnp.logical_not(source))
                def _():
                    remote(piece, piece, t1_s.at[0, 0], t1_r, row, y).wait_recv()

                for d in range(1, NY):
                    remote(piece, piece, t2_s.at[d], t2_r.at[y], row, x * NY + (y + d) % NY).start()

        if tick == AT_T:
            for j in range(3):
                @pl.when(y != j)
                def _(j=j):
                    piece = TG.at[c, z, j]
                    remote(piece, piece, t2_s.at[0], t2_r.at[j], row, q).wait_recv()
        if AT_T <= tick <= AT_T + n_t:
            ag_step("t", T_WAY, T_CUT, tmine, tick - AT_T, tg_s, tg_r, to_sibling(tmine, ft_s, ft_r))
        if tick == AT_D:
            @pl.when(z != 0)
            def _():
                remote(B.at[:, 0:ch], DG.at[z, pl.ds(0, 2)], ds_s.at[0], ds_r.at[0], up, q).wait_recv()

            @pl.when(z != 1)
            def _():
                remote(
                    B.at[pl.ds(0, 1), 0:ch], DG.at[z, pl.ds(2, 1)], ds_s.at[0], ds_r.at[1], up, q
                ).wait_recv()
        if AT_D <= tick <= AT_D + n_d:
            ag_step("d", D_WAY, D_CUT, DG, tick - AT_D, dg_s, dg_r)
        if AT_S <= tick <= AT_S + n_s:
            ag_step("s", S_WAY, S_CUT, smine, tick - AT_S, sg_s, sg_r, to_sibling(smine, fs_s, fs_r))
        if tick == at_x:
            dg = [split3(DG[:, k].reshape(nb, nb)) for k in range(3)]
            for h in range(2):
                moved = jnp.zeros((nb, nb), F32)
                for k in range(3):
                    oh = jnp.broadcast_to(came[h], (nb, nb)) == lanef + float(k * nb)
                    oh = oh.astype(F32).astype(BF16)
                    moved += dot(oh, dg[k][0]) + dot(oh, dg[k][1]) + dot(oh, dg[k][2])
                keep = jnp.broadcast_to(came[h], (nb, nb)) == jnp.broadcast_to(own[h], (nb, nb))
                NBf[h] = jnp.where(keep, B[h], moved)

                @pl.when(source)
                def _(h=h):
                    for cp in strips(h):
                        cp.start()
                    if h == 0:
                        XG[y] = NBf[0]

            crossing.append(begin(remote(NBf.at[1 - c], NX_, nx_s, nx_r, sib, q)))
        for p in range(PX):
            if tick == AT_X2 + p * GAP_X // PX:
                @pl.when(y < 3)
                def _(p=p):
                    piece = XG.at[y, part(p)]

                    @pl.when(jnp.logical_not(source))
                    def _():
                        remote(piece, piece, x1_s.at[0, 0, p], x1_r.at[p], row, y).wait_recv()

                    for d in range(1, NY):
                        strips_y(d, p).start()

    for cp in crossing:
        cp.wait_recv()

    load_inv.wait()
    i0, i1, i2 = inv_ref[0], inv_ref[1], inv_ref[2]
    t10, t01, t02, t20, t21, t12 = (TG[j // 3, :, j % 3].reshape(nb, nb) for j in range(6))
    l10, l20 = mm(t10, i0), mm(t20, i0)
    l21 = mm(t21 - mm(l20, t01), i1)
    u12 = t12 - mm(l10, t02)
    us = []
    for h in range(2):
        s0, s1, s2 = (SG[h, :, k].reshape(nb, nb) for k in range(3))
        u1 = s1 - mm(l10, s0)
        us.append((s0, u1, s2 - mm(l20, s0) - mm(l21, u1)))

    for j in range(3):
        @pl.when(y != j)
        def _(j=j):
            for p in range(PX):
                piece = XG.at[j, part(p)]
                remote(piece, piece, x2_s.at[0, p], x2_r.at[j, p], row, q).wait_recv()
    l0 = mm(XG[0], i0)
    l1 = mm(XG[1] - mm(l0, t01), i1)
    l2 = mm(XG[2] - mm(l0, t02) - mm(l1, u12), i2)
    for h in range(2):
        cols = pl.ds(h * nb, nb)
        u0, u1, u2 = us[h]

        @pl.when(row >= 3)
        def _(h=h, cols=cols, u0=u0, u1=u1, u2=u2):
            @pl.when(c == h)
            def _():
                o_ref[:, cols] = NBf[h]

            @pl.when(c != h)
            def _():
                o_ref[:, cols] = NX_[...]

            o_ref[:, cols] -= mm(l0, u0) + mm(l1, u1) + mm(l2, u2)

        for r, u in enumerate((u0, u1, u2)):
            @pl.when(row == r)
            def _(cols=cols, u=u):
                o_ref[:, cols] = u
    for k, l in enumerate((l0, l1, l2)):
        @pl.when(jnp.logical_and(row >= 3, q == k))
        def _(l=l):
            o_ref[:, 0:nb] = l
    for r, k, l in ((1, 0, l10), (2, 0, l20), (2, 1, l21)):
        @pl.when(jnp.logical_and(row == r, q == k))
        def _(l=l):
            o_ref[:, 0:nb] = l

    swap.wait_send()
    for cp in sent:
        cp.wait_send()
    for which in range(2):
        @pl.when(z == which)
        def _(which=which):
            for d in range(1, nz):
                share(which, d).wait_send()

    @pl.when(source)
    def _():
        for d in range(1, NX):
            remote(SG.at[0, z, 0], TG.at[0, z, y], t1_s.at[0, d], t1_r, 2 * z, d * NY + y).wait_send()
        for d in range(NX):
            remote(SG.at[0, z, 0], TG.at[1, z, y], t1_s.at[1, d], t1_r, 2 * z + 1, d * NY + y).wait_send()
        for h in range(2):
            for cp in strips(h):
                cp.wait_send()

    @pl.when(y < 3)
    def _():
        for d in range(1, NY):
            to = x * NY + (y + d) % NY
            piece = TG.at[c, z, y]
            remote(piece, piece, t2_s.at[d], t2_r.at[y], row, to).wait_send()
            for p in range(PX):
                strips_y(d, p).wait_send()


def on_device(matrix, pivots, inverses):
    nb = inverses.shape[1]
    nz = lax.axis_size("row") // 2
    ch = nb // nz
    DMA = pltpu.SemaphoreType.DMA

    def vm(*shape):
        return pltpu.VMEM(shape, F32)

    return pl.pallas_call(
        functools.partial(kernel, nz, nb),
        out_shape=jax.ShapeDtypeStruct(matrix.shape, matrix.dtype),
        in_specs=[
            pl.BlockSpec(memory_space=pl.ANY),
            pl.BlockSpec(memory_space=pl.ANY),
            pl.BlockSpec(memory_space=pl.ANY),
        ],
        out_specs=pl.BlockSpec(memory_space=pltpu.VMEM),
        scratch_shapes=[
            pltpu.VMEM(pivots.shape, jnp.int32), vm(*inverses.shape), DMA((2,)),
            vm(2, nb, nb), vm(nz, 3, ch, nb), vm(2, nz, 3, ch, nb), vm(nz, 3, ch, nb), vm(2, nz, 3, ch, nb),
            vm(3, nb, nb), vm(2, nb, nb), vm(nb, nb),
            vm(nz - 1, 3, ch, nb), vm(nz - 1, 3, ch, nb),
            DMA, DMA, DMA, DMA((nz,)), DMA((2,)),
            DMA((nz - 1, 3)), DMA((nz - 1, 3)), DMA((nz - 1, 3)), DMA((nz - 1, 3)),
            DMA((nz - 1, 3)), DMA((nz - 1, 3)), DMA((nz - 1, 3)), DMA((nz - 1, 3)),
            DMA((nz,)), DMA((nz,)), DMA((nz,)), DMA((nz,)),
            DMA((2, NX)), DMA, DMA((NY,)), DMA((3,)),
            DMA((2, NX, PX)), DMA((PX,)), DMA((NY, PX)), DMA((3, PX)),
            DMA, DMA,
        ],
        compiler_params=pltpu.CompilerParams(
            collective_id=0, has_side_effects=True, vmem_limit_bytes=60 * 2**20
        ),
        name="panels",
    )(matrix, pivots, inverses)


def solution(mesh):
    placed = (P("row", "col"), P(), P())
    return jax.shard_map(
        on_device, mesh=mesh, in_specs=placed, out_specs=P("row", "col"), check_vma=False
    )
```
